32 devices in a mesh: groups: 1, dp: 1, tensor: 32 (over z, y, x, core).
Axes of the slice: x: 2, y: 2, z: 4, core: 2. Of those that a mesh axis runs over, the one named last changes fastest.
Arguments:
- queries: bfloat16 [128, 8192], P(('groups', 'dp'), 'tensor'), may hold values from -200 to 200
- cache: bfloat16 [32, 128, 128, 256], P('tensor', ('groups', 'dp')), may hold values from -6 to 6, as said below
- lengths: int32 [128], P(('groups', 'dp')), may hold values from 2 to 128, as said below
- request_adapter_index: int32 [128], P(('groups', 'dp')), may hold values from 0 to 7
- output_projection_weight: bfloat16 [8192, 8192], P('tensor'), may hold values from -0.125 to 0.125
- adapter_down_weight: bfloat16 [8, 8192, 64], P(('groups', 'dp'), 'tensor'), may hold values from -0.0625 to 0.0625
- adapter_up_weight: bfloat16 [8, 64, 8192], P(('groups', 'dp'), None, 'tensor'), may hold values from -0.75 to 0.75
Outputs:
- mixed: bfloat16 [8192, 128], P('tensor', ('groups', 'dp'))
The draws below stay inside these ranges and needn't reach their ends.
Inputs may be any that keep to these rules, and one draw needn't show every extreme that they name: `lengths`: in each dp index's 128 requests at least one has length 128. `cache`: copies i and j are equal where i // 4 == j // 4.
All inputs are finite; a program needn't handle non-finite values.
Results may differ from the reference program's by a relative error of at most 0.006.
Values may be sent and summed in bfloat16 or wider, within the bound.
A program may use at most 64 MiB of HBM per device.

```python
import math
import jax
import jax.numpy as jnp
from jax import lax

HEADS = 64
HEAD = 128
KV_HEADS = 8
MODEL_WIDTH = 8192
ADAPTER_RANK = 64
REQ_DEV = 128
CTX = 128
REQS = 128
ADAPTER_TOTAL = 8
KV_COPIES = 32


def shared_cache(key):
    base = jnp.clip(jax.random.normal(key, (KV_HEADS, REQS, CTX, 2 * HEAD), jnp.float32), -6.0, 6.0)
    return base


def draw_cache(key, part):
    return jnp.repeat(shared_cache(key), KV_COPIES // KV_HEADS, axis=0).astype(jnp.bfloat16)


def draw_queries(key, part):
    own_key = jax.random.fold_in(key, 7)
    values = jnp.clip(jax.random.normal(own_key, (REQS, HEADS, HEAD), jnp.float32), -6.0, 6.0)
    return values.reshape(REQS, HEADS * HEAD).astype(jnp.bfloat16)


def draw_lengths(key, part):
    key = jax.random.fold_in(key, 11)
    first_key, second_key = jax.random.split(key)
    drawn = jax.random.randint(first_key, (REQS,), 2, CTX + 1)
    picks = jax.random.randint(second_key, (REQS // REQ_DEV,), 0, REQ_DEV)
    request = jnp.arange(REQS)
    chosen = request % REQ_DEV == jnp.repeat(picks, REQ_DEV)
    return jnp.where(chosen, CTX, drawn).astype(jnp.int32)


def plant(values, key, smallest, top_value):
    dims = values.shape
    place = [jax.random.randint(jax.random.fold_in(key, axis), (), 0, dims[axis]) for axis in range(len(dims))]
    values = values.at[tuple(place)].set(smallest)
    longest = dims.index(max(dims))
    place[longest] = (place[longest] + 1) % dims[longest]
    return values.at[tuple(place)].set(top_value)


def raised(entries, stream_key, source, target, parts, factor):
    def block_of(position):
        return (jnp.arange(entries.shape[position]) // (entries.shape[position] // parts)).reshape((-1,) + (1,) * (entries.ndim - 1 - position))

    one_side = jax.random.permutation(stream_key, parts)[block_of(target)]
    other_side = (block_of(target) + parts // 2) % parts
    return jnp.where((block_of(source) == one_side) | (block_of(source) == other_side), factor * entries, entries)


def steps_of(key, extent, pieces, smallest, largest):
    loudness, own = 1.0, jax.random.fold_in(key, 6)
    for axis_at, shards_of in pieces:
        draws = jnp.exp(jax.random.uniform(jax.random.fold_in(own, axis_at), (shards_of,), jnp.float32, smallest / len(pieces), largest / len(pieces)))
        loudness = loudness * jnp.repeat(draws, extent[axis_at] // shards_of).reshape([-1 if axis == axis_at else 1 for axis in range(len(extent))])
    return loudness


def scatter_about(stream_key, extent, scale, bound, cuts=(), held_as=jnp.bfloat16):
    entries = jax.random.normal(stream_key, extent, jnp.float32) * scale
    if len(cuts) > 0:
        entries = steps_of(stream_key, extent, cuts, -0.22, 0.18) * entries
    return jnp.clip(entries, min=-bound, max=bound).astype(held_as)


def noise_with(key, extent, deviation, bound, cuts, heavy, kind=jnp.bfloat16):
    array = deviation * jax.random.normal(key, extent, jnp.float32)
    if cuts:
        array = array * steps_of(key, extent, cuts, -0.22, 0.18)
    return jnp.clip(raised(array, jax.random.fold_in(key, 3), *heavy), -bound, bound).astype(kind)


def setup_inputs(seed: int = 0, part: int = 0) -> dict:
    arg_keys = jax.random.split(jax.random.key(seed), 8)
    part_keys = jax.random.split(jax.random.fold_in(arg_keys[7], part), 8)
    queries = draw_queries(jax.random.fold_in(jax.random.fold_in(arg_keys[7], part), 71), part)
    cache = draw_cache(jax.random.fold_in(jax.random.fold_in(arg_keys[7], part), 71), part)
    lengths = draw_lengths(jax.random.fold_in(jax.random.fold_in(arg_keys[7], part), 71), part)
    request_adapter_index = plant(jax.random.randint(part_keys[3], (REQS,), 0, ADAPTER_TOTAL), jax.random.fold_in(part_keys[3], 1), 0, ADAPTER_TOTAL - 1).astype(jnp.int32)
    output_projection_weight = noise_with(arg_keys[4], (MODEL_WIDTH, MODEL_WIDTH), MODEL_WIDTH ** -0.5, 0.125, ((0, 32),), (0, 1, 32, 2.75))
    adapter_down_weight = scatter_about(part_keys[5], (ADAPTER_TOTAL, MODEL_WIDTH, ADAPTER_RANK), MODEL_WIDTH ** -0.5, 0.0625, ((1, 32),))
    adapter_up_weight = scatter_about(part_keys[6], (ADAPTER_TOTAL, ADAPTER_RANK, MODEL_WIDTH), ADAPTER_RANK ** -0.5, 0.75, ((2, 32),))
    return {"queries": queries, "cache": cache, "lengths": lengths, "request_adapter_index": request_adapter_index, "output_projection_weight": output_projection_weight, "adapter_down_weight": adapter_down_weight, "adapter_up_weight": adapter_up_weight}


def reference(queries, cache, lengths, request_adapter_index, output_projection_weight, adapter_down_weight, adapter_up_weight):
    per_kv = HEADS // KV_HEADS
    spread = KV_COPIES // KV_HEADS
    scale = 1.0 / math.sqrt(HEAD)
    live = jnp.arange(CTX)[None, :] < lengths[:, None]

    def one_head(adapter_index):
        start = (adapter_index * per_kv * HEAD).astype(jnp.int32)
        grouped = lax.dynamic_slice_in_dim(queries, start, per_kv * HEAD, 1)
        grouped = grouped.reshape(REQS, per_kv, HEAD).astype(jnp.float32)
        slots = cache[adapter_index * spread].astype(jnp.float32)
        scores = jnp.einsum('rhe,rte->rht', grouped, slots[:, :, :HEAD]) * scale
        scores = jnp.where(live[:, None, :], scores, jnp.float32(-1e+30))
        top = lax.optimization_barrier(jnp.max(scores, axis=-1, keepdims=True))
        expd = jnp.exp(scores - top)
        weights = (expd / lax.optimization_barrier(jnp.sum(expd, axis=-1, keepdims=True))).astype(jnp.bfloat16)
        weights = lax.optimization_barrier(weights).astype(jnp.float32)
        mixed_heads = jnp.einsum('rht,rte->rhe', weights, slots[:, :, HEAD:])
        return mixed_heads.astype(jnp.bfloat16).reshape(REQS, per_kv * HEAD)
    heads_out = lax.map(one_head, jnp.arange(KV_HEADS, dtype=jnp.int32))
    attended_state = jnp.transpose(heads_out, (1, 0, 2)).reshape(REQS, MODEL_WIDTH)

    def down_step(carry, adapter_index):
        adapter_correction = jnp.dot(attended_state, adapter_down_weight[adapter_index], preferred_element_type=jnp.float32)
        return (jnp.where((request_adapter_index == adapter_index)[:, None], adapter_correction, carry), None)
    low_rank_state, _ = lax.scan(down_step, jnp.zeros((REQS, ADAPTER_RANK), jnp.float32), jnp.arange(ADAPTER_TOTAL, dtype=jnp.int32))
    low_rank_state = low_rank_state.astype(jnp.bfloat16)

    def up_step(carry, adapter_index):
        adapter_correction = jnp.dot(low_rank_state, adapter_up_weight[adapter_index], preferred_element_type=jnp.float32)
        return (jnp.where((request_adapter_index == adapter_index)[:, None], adapter_correction, carry), None)
    delta, _ = lax.scan(up_step, jnp.zeros((REQS, MODEL_WIDTH), jnp.float32), jnp.arange(ADAPTER_TOTAL, dtype=jnp.int32))
    base = jnp.dot(attended_state, output_projection_weight, preferred_element_type=jnp.float32)
    return jnp.transpose(base + delta).astype(jnp.bfloat16)
```

```python
import math

import jax
import jax.numpy as jnp
from jax import lax
from jax.experimental import pallas as pl
from jax.experimental.pallas import tpu as pltpu
from jax.sharding import PartitionSpec as P

HEAD = 128
PIECES = 2
CHUNK = 16
MESH = pl.DeviceIdType.MESH
F32 = jnp.float32
BF16 = jnp.bfloat16
NEG = -1e30


def kernel(
    q_ref, len_ref, idx_ref, cache_hbm, w_hbm, down_hbm, up_hbm, out_ref,
    cache, w, down, up, lens, picks, att,
    sent1, own, got1, sent2, kept1, got2, sent3, kept2, got3, sent4, got4,
    low0, low1, low2, low3, lg1, lg2, lg3, lg4,
    load_sem, send_sem, recv_sem,
):
    rows = q_ref.shape[0]
    half = rows // PIECES
    chunks = rows // CHUNK
    slots = cache.shape[1]
    count = down.shape[0]
    rank = down.shape[2]
    out_width = up.shape[2]

    me = lax.axis_index("tensor")
    core = me % 2
    xx = (me // 2) % 2
    yy = (me // 4) % 2
    zz = me // 8
    core_peer = me + 1 - 2 * core
    x_peer = me + 2 - 4 * xx
    y_peer = me + 4 - 8 * yy
    z_others = (zz + 1 - 2 * (zz % 2), (zz + 2) % 4, 3 - zz)
    z_peers = tuple(me + 8 * (other - zz) for other in z_others)
    peers = (core_peer, x_peer, y_peer) + z_peers

    cache_loads = [
        pltpu.make_async_copy(
            cache_hbm.at[0, pl.ds(c * CHUNK, CHUNK)],
            cache.at[pl.ds(c * CHUNK, CHUNK)],
            load_sem.at[c],
        )
        for c in range(chunks)
    ]
    down_load = pltpu.make_async_copy(down_hbm, down, load_sem.at[chunks])
    up_load = pltpu.make_async_copy(up_hbm, up, load_sem.at[chunks + 1])
    w_load = pltpu.make_async_copy(w_hbm, w, load_sem.at[chunks + 2])
    for c in range(chunks // 2):
        cache_loads[c].start()
    down_load.start()
    w_load.start()
    for c in range(chunks // 2, chunks):
        cache_loads[c].start()
    up_load.start()

    barrier = pltpu.get_barrier_semaphore()
    for peer in peers:
        pl.semaphore_signal(barrier, inc=1, device_id={"tensor": peer}, device_id_type=MESH)

    def send(p, step, src, dst, peer):
        return pltpu.make_async_remote_copy(
            src_ref=src,
            dst_ref=dst,
            send_sem=send_sem.at[p, step],
            recv_sem=recv_sem.at[p, step],
            device_id={"tensor": peer},
            device_id_type=MESH,
        )

    lens[...] = jnp.transpose(jnp.broadcast_to(len_ref[...].astype(F32), (slots, rows)))
    picks[...] = jnp.transpose(jnp.broadcast_to(idx_ref[...].astype(F32), (out_width, rows)))

    row_of = lax.broadcasted_iota(jnp.int32, (2 * CHUNK, slots), 0) % CHUNK
    slot_of = lax.broadcasted_iota(jnp.int32, (2 * CHUNK, slots), 1).astype(F32)
    scale = 1.0 / math.sqrt(HEAD)

    def attend(c, carry):
        at = pl.multiple_of(c * CHUNK, CHUNK)
        pltpu.make_async_copy(
            cache_hbm.at[0, pl.ds(at, CHUNK)], cache.at[pl.ds(at, CHUNK)], load_sem.at[c]
        ).wait()
        block = cache[pl.ds(at, CHUNK)].reshape(CHUNK * slots, 2 * HEAD)
        q = q_ref[pl.ds(at, CHUNK), :]
        q = jnp.concatenate([q[:, :HEAD], q[:, HEAD:]], axis=0)
        raw = lax.dot_general(
            q, block[:, :HEAD], (((1,), (1,)), ((), ())), preferred_element_type=F32
        )
        scores = raw[:, :slots]
        for r in range(1, CHUNK):
            scores = jnp.where(row_of == r, raw[:, r * slots : (r + 1) * slots], scores)
        live = lens[pl.ds(at, CHUNK), :]
        live = jnp.concatenate([live, live], axis=0)
        scores = jnp.where(slot_of < live, scores * scale, NEG)
        top = jnp.max(scores, axis=-1, keepdims=True)
        expd = jnp.exp(scores - top)
        weights = expd / jnp.sum(expd, axis=-1, keepdims=True)
        spread = jnp.concatenate(
            [jnp.where(row_of == r, weights, 0.0).astype(BF16) for r in range(CHUNK)], axis=1
        )
        mixed = jnp.dot(spread, block[:, HEAD:], preferred_element_type=F32).astype(BF16)
        att[pl.ds(at, CHUNK), :HEAD] = mixed[:CHUNK]
        att[pl.ds(at, CHUNK), HEAD:] = mixed[CHUNK:]
        return carry

    def fold(low):
        return jnp.concatenate([low[: half // 2], low[half // 2 :]], axis=1)

    def unfold(low):
        return jnp.concatenate([low[:, :rank], low[:, rank:]], axis=0)

    first_peer = (x_peer, y_peer)
    second_peer = (y_peer, x_peer)
    first = (xx, yy)
    second = (yy, xx)
    first_step = (2, 4)
    second_step = (4, 2)

    def columns(p, i, side):
        index = (i % 4) * 8 + (i // 8) * first_step[p] + ((i // 4) % 2) * second_step[p] + side
        return pl.ds(pl.multiple_of(index * out_width, out_width), out_width)

    def low_part(p):
        piece = att[p * half : (p + 1) * half, :].astype(F32)
        pick = picks[p * half : (p + 1) * half, :]
        total = jnp.zeros((half, rank), F32)
        for a in range(count):
            chosen = jnp.where(pick == a, piece, 0.0).astype(BF16)
            total = total + jnp.dot(chosen, down[a], preferred_element_type=F32)
        low0[p] = fold(total)
        copy = send(p, 6, low0.at[p], lg1.at[p], core_peer)
        copy.start()
        return copy

    def project(p):
        def far(i, carry):
            sent1[p, i] = jnp.dot(
                att[p * half : (p + 1) * half, :], w[:, columns(p, i, 1 - core)],
                preferred_element_type=F32,
            ).astype(BF16)
            return carry

        def near(i, carry):
            own[p, i] = jnp.dot(
                att[p * half : (p + 1) * half, :], w[:, columns(p, i, core)],
                preferred_element_type=F32,
            )
            return carry

        lax.fori_loop(0, 16, far, 0)
        copy = send(p, 0, sent1.at[p], got1.at[p], core_peer)
        copy.start()
        lax.fori_loop(0, 16, near, 0)
        return copy

    def along_first(p, copy, low_copy):
        low_copy.wait()
        low1[p] = low0[p] + lg1[p]
        low_next = send(p, 7, low1.at[p], lg2.at[p], first_peer[p])
        low_next.start()
        copy.wait()
        mine, other = first[p] * 8, (1 - first[p]) * 8

        def give(j, carry):
            sent2[p, j] = (own[p, other + j] + got1[p, other + j].astype(F32)).astype(BF16)
            return carry

        def keep(j, carry):
            kept1[p, j] = own[p, mine + j] + got1[p, mine + j].astype(F32)
            return carry

        lax.fori_loop(0, 8, give, 0)
        following = send(p, 1, sent2.at[p], got2.at[p], first_peer[p])
        following.start()
        lax.fori_loop(0, 8, keep, 0)
        return following, low_next

    def along_second(p, copy, low_copy):
        low_copy.wait()
        low2[p] = low1[p] + lg2[p]
        low_next = send(p, 8, low2.at[p], lg3.at[p], second_peer[p])
        low_next.start()
        copy.wait()
        mine, other = second[p] * 4, (1 - second[p]) * 4

        def give(j, carry):
            sent3[p, j] = (kept1[p, other + j] + got2[p, other + j].astype(F32)).astype(BF16)
            return carry

        def keep(j, carry):
            kept2[p, j] = kept1[p, mine + j] + got2[p, mine + j].astype(F32)
            return carry

        lax.fori_loop(0, 4, give, 0)
        following = send(p, 2, sent3.at[p], got3.at[p], second_peer[p])
        following.start()
        lax.fori_loop(0, 4, keep, 0)
        return following, low_next

    def along_z(p, copy, low_copy):
        low_copy.wait()
        low3[p] = low2[p] + lg3[p]
        copies = []
        for k in range(3):
            copies.append(send(p, 9 + k, low3.at[p], lg4.at[p, k], z_peers[k]))
            copies[-1].start()
        copy.wait()
        for k in (1, 2, 0):
            to = z_others[k]
            sent4[p, k] = (kept2[p, to] + got3[p, to].astype(F32)).astype(BF16)
            copies.append(send(p, 3 + k, sent4.at[p, k], got4.at[p, k], z_peers[k]))
            copies[-1].start()
        return copies

    def finish(p, copies):
        for copy in copies[:3]:
            copy.wait()
        low = unfold(low3[p] + lg4[p, 0] + (lg4[p, 1] + lg4[p, 2]))
        low = low.astype(BF16).astype(F32)
        pick = picks[p * half : (p + 1) * half, :rank]
        total = kept2[p, zz] + got3[p, zz].astype(F32)
        for a in range(count):
            chosen = jnp.where(pick == a, low, 0.0).astype(BF16)
            total = total + jnp.dot(chosen, up[a], preferred_element_type=F32)
        for copy in copies[3:]:
            copy.wait()
        for k in range(3):
            total = total + got4[p, k].astype(F32)
        return total

    lax.fori_loop(0, chunks // 2, attend, 0)
    down_load.wait()
    pl.semaphore_wait(barrier, len(peers))
    low_a = low_part(0)
    w_load.wait()
    a = project(0)
    lax.fori_loop(chunks // 2, chunks, attend, 0)
    low_b = low_part(1)
    a, low_a = along_first(0, a, low_a)
    b = project(1)
    b, low_b = along_first(1, b, low_b)
    a, low_a = along_second(0, a, low_a)
    b, low_b = along_second(1, b, low_b)
    a = along_z(0, a, low_a)
    b = along_z(1, b, low_b)
    up_load.wait()
    top = finish(0, a)
    bottom = finish(1, b)
    out_ref[...] = jnp.transpose(jnp.concatenate([top, bottom], axis=0)).astype(BF16)


def body(
    queries,
    cache,
    lengths,
    request_adapter_index,
    output_projection_weight,
    adapter_down_weight,
    adapter_up_weight,
):
    downs, ups = (
        lax.all_gather(adapter_down_weight, "dp", axis=0, tiled=True),
        lax.all_gather(adapter_up_weight, "dp", axis=0, tiled=True),
    )
    rows = queries.shape[0]
    half = rows // PIECES
    chunks = rows // CHUNK
    slots = cache.shape[2]
    width = ups.shape[2]
    rank = downs.shape[2]
    low = (PIECES, half // 2, 2 * rank)

    def blocks(n, kind=BF16):
        return pltpu.VMEM((PIECES, n, half, width), kind)

    vmem = pl.BlockSpec(memory_space=pltpu.VMEM)
    hbm = pl.BlockSpec(memory_space=pl.ANY)
    return pl.pallas_call(
        kernel,
        out_shape=jax.ShapeDtypeStruct((width, rows), BF16),
        in_specs=[vmem, vmem, vmem, hbm, hbm, hbm, hbm],
        out_specs=vmem,
        scratch_shapes=[
            pltpu.VMEM(cache.shape[1:], BF16),
            pltpu.VMEM(output_projection_weight.shape, BF16),
            pltpu.VMEM(downs.shape, BF16),
            pltpu.VMEM(ups.shape, BF16),
            pltpu.VMEM((rows, slots), F32),
            pltpu.VMEM((rows, width), F32),
            pltpu.VMEM((rows, queries.shape[1]), BF16),
            blocks(16), blocks(16, F32), blocks(16),
            blocks(8), blocks(8, F32), blocks(8),
            blocks(4), blocks(4, F32), blocks(4),
            blocks(3), blocks(3),
            pltpu.VMEM(low, F32), pltpu.VMEM(low, F32), pltpu.VMEM(low, F32), pltpu.VMEM(low, F32),
            pltpu.VMEM(low, F32), pltpu.VMEM(low, F32), pltpu.VMEM(low, F32),
            pltpu.VMEM((PIECES, 3) + low[1:], F32),
            pltpu.SemaphoreType.DMA((chunks + 3,)),
            pltpu.SemaphoreType.DMA((PIECES, 12)),
            pltpu.SemaphoreType.DMA((PIECES, 12)),
        ],
        compiler_params=pltpu.CompilerParams(
            collective_id=0, has_side_effects=True, vmem_limit_bytes=48 * 1024 * 1024
        ),
    )(
        queries,
        lengths.reshape(1, rows),
        request_adapter_index.reshape(1, rows),
        cache,
        output_projection_weight,
        downs,
        ups,
    )


def solution(mesh):
    return jax.shard_map(
        body,
        mesh=mesh,
        in_specs=(
            P(("groups", "dp"), "tensor"),
            P("tensor", ("groups", "dp"), None, None),
            P(("groups", "dp")),
            P(("groups", "dp")),
            P("tensor", None),
            P(("groups", "dp"), "tensor", None),
            P(("groups", "dp"), None, "tensor"),
        ),
        out_specs=P("tensor", ("groups", "dp")),
        check_vma=False,
    )
```

```python
import math

import jax
import jax.numpy as jnp
from jax import lax
from jax.experimental import pallas as pl
from jax.experimental.pallas import tpu as pltpu
from jax.sharding import PartitionSpec as P

HEAD = 128
PIECES = 2
CHUNK = 16
MESH = pl.DeviceIdType.MESH
F32 = jnp.float32
BF16 = jnp.bfloat16
NEG = -1e30


def kernel(
    q_hbm, len_hbm, idx_hbm, cache_hbm, w_hbm, down_hbm, up_hbm, out_ref,
    q_ref, len_ref, idx_ref, cache, w, down, up, lens, picks, att,
    sent1, own, got1, sent2, kept1, got2, sent3, kept2, got3, sent4, got4,
    low0, low1, low2, low3, lg1, lg2, lg3, lg4,
    load_sem, send_sem, recv_sem,
):
    rows = q_hbm.shape[0]
    half = rows // PIECES
    chunks = rows // CHUNK
    slots = cache.shape[1]
    count = down.shape[0]
    rank = down.shape[1]
    out_width = up.shape[2]

    me = lax.axis_index("tensor")
    core = me % 2
    xx = (me // 2) % 2
    yy = (me // 4) % 2
    zz = me // 8
    core_peer = me + 1 - 2 * core
    x_peer = me + 2 - 4 * xx
    y_peer = me + 4 - 8 * yy
    z_others = (zz + 1 - 2 * (zz % 2), (zz + 2) % 4, 3 - zz)
    z_peers = tuple(me + 8 * (other - zz) for other in z_others)
    peers = (core_peer, x_peer, y_peer) + z_peers

    cache_loads = [
        pltpu.make_async_copy(
            cache_hbm.at[0, pl.ds(c * CHUNK, CHUNK)],
            cache.at[pl.ds(c * CHUNK, CHUNK)],
            load_sem.at[c],
        )
        for c in range(chunks)
    ]
    down_load = pltpu.make_async_copy(down_hbm, down, load_sem.at[chunks])
    up_load = pltpu.make_async_copy(up_hbm, up, load_sem.at[chunks + 1])
    w_load = pltpu.make_async_copy(w_hbm, w, load_sem.at[chunks + 2])
    small_loads = [
        pltpu.make_async_copy(src, dst, load_sem.at[chunks + 3 + i])
        for i, (src, dst) in enumerate(((q_hbm, q_ref), (len_hbm, len_ref), (idx_hbm, idx_ref)))
    ]
    for load in small_loads:
        load.start()
    for c in range(chunks // 2):
        cache_loads[c].start()
    down_load.start()
    w_load.start()
    for c in range(chunks // 2, chunks):
        cache_loads[c].start()
    up_load.start()

    barrier = pltpu.get_barrier_semaphore()
    for peer in peers:
        pl.semaphore_signal(barrier, inc=1, device_id={"tensor": peer}, device_id_type=MESH)

    def send(p, step, src, dst, peer):
        return pltpu.make_async_remote_copy(
            src_ref=src,
            dst_ref=dst,
            send_sem=send_sem.at[p, step],
            recv_sem=recv_sem.at[p, step],
            device_id={"tensor": peer},
            device_id_type=MESH,
        )

    for load in small_loads:
        load.wait()
    lens[...] = jnp.transpose(jnp.broadcast_to(len_ref[...].astype(F32), (slots, rows)))
    picks[...] = jnp.transpose(jnp.broadcast_to(idx_ref[...].astype(F32), (out_width, rows)))

    row_of = lax.broadcasted_iota(jnp.int32, (2 * CHUNK, slots), 0) % CHUNK
    slot_of = lax.broadcasted_iota(jnp.int32, (2 * CHUNK, slots), 1).astype(F32)
    scale = 1.0 / math.sqrt(HEAD)

    def attend(c, carry):
        at = pl.multiple_of(c * CHUNK, CHUNK)
        pltpu.make_async_copy(
            cache_hbm.at[0, pl.ds(at, CHUNK)], cache.at[pl.ds(at, CHUNK)], load_sem.at[c]
        ).wait()
        block = cache[pl.ds(at, CHUNK)].reshape(CHUNK * slots, 2 * HEAD)
        q = q_ref[pl.ds(at, CHUNK), :]
        q = jnp.concatenate([q[:, :HEAD], q[:, HEAD:]], axis=0)
        raw = lax.dot_general(
            q, block[:, :HEAD], (((1,), (1,)), ((), ())), preferred_element_type=F32
        )
        scores = raw[:, :slots]
        for r in range(1, CHUNK):
            scores = jnp.where(row_of == r, raw[:, r * slots : (r + 1) * slots], scores)
        live = lens[pl.ds(at, CHUNK), :]
        live = jnp.concatenate([live, live], axis=0)
        scores = jnp.where(slot_of < live, scores * scale, NEG)
        top = jnp.max(scores, axis=-1, keepdims=True)
        expd = jnp.exp(scores - top)
        weights = expd / jnp.sum(expd, axis=-1, keepdims=True)
        spread = jnp.concatenate(
            [jnp.where(row_of == r, weights, 0.0).astype(BF16) for r in range(CHUNK)], axis=1
        )
        mixed = jnp.dot(spread, block[:, HEAD:], preferred_element_type=F32).astype(BF16)
        att[pl.ds(at, CHUNK), :HEAD] = mixed[:CHUNK]
        att[pl.ds(at, CHUNK), HEAD:] = mixed[CHUNK:]
        return carry

    def fold(low):
        return jnp.concatenate([low[: half // 2], low[half // 2 :]], axis=1)

    def unfold(low):
        return jnp.concatenate([low[:, :rank], low[:, rank:]], axis=0)

    first_peer = (x_peer, y_peer)
    second_peer = (y_peer, x_peer)
    z_order = (z_others[1], z_others[2], z_others[0], zz)
    z_slot_peers = (z_peers[1], z_peers[2], z_peers[0])

    def group_of(p, dx, dy):
        return dx * 2 + dy if p == 0 else dy * 2 + dx

    def low_part(p):
        piece = att[p * half : (p + 1) * half, :].astype(F32)
        pick = picks[p * half : (p + 1) * half, :]
        total = jnp.zeros((half, rank), F32)
        for a in range(count):
            chosen = jnp.where(pick == a, piece, 0.0).astype(BF16)
            total = total + lax.dot_general(
                chosen, down[a], (((1,), (1,)), ((), ())), preferred_element_type=F32
            )
        low0[p] = fold(total)
        copy = send(p, 6, low0.at[p], lg1.at[p], core_peer)
        copy.start()
        return copy

    def product(dx, dy, side, slot):
        x_at = xx + dx * (1 - 2 * xx)
        y_at = yy + dy * (1 - 2 * yy)
        index = z_order[slot] * 8 + y_at * 4 + x_at * 2 + side
        columns = pl.ds(pl.multiple_of(index * out_width, out_width), out_width)
        return jnp.dot(att[...], w[:, columns], preferred_element_type=F32)

    def far(dx, dy):
        places = (group_of(0, dx, dy), group_of(1, dx, dy))
        for slot in range(4):
            block = product(dx, dy, 1 - core, slot).astype(BF16)
            for p in range(PIECES):
                sent1[p, places[p] * 4 + slot] = block[p * half : (p + 1) * half]
        copies = []
        for p in range(PIECES):
            at = pl.ds(places[p] * 4, 4)
            copies.append(send(p, 12 + places[p], sent1.at[p, at], got1.at[p, at], core_peer))
            copies[-1].start()
        return copies

    def near(dx, dy, copies):
        places = (group_of(0, dx, dy), group_of(1, dx, dy))
        for slot in range(4):
            block = product(dx, dy, core, slot)
            for p in range(PIECES):
                own[p, places[p] * 4 + slot] = block[p * half : (p + 1) * half]
        following = [None] * PIECES
        for p in range(PIECES):
            place = places[p]
            copies[p].wait()
            to = (place % 2) * 4
            for slot in range(4):
                total = own[p, place * 4 + slot] + got1[p, place * 4 + slot].astype(F32)
                if place >= 2:
                    sent2[p, to + slot] = total.astype(BF16)
                else:
                    kept1[p, to + slot] = total
            if place >= 2:
                at = pl.ds(to, 4)
                following[p] = send(p, place % 2, sent2.at[p, at], got2.at[p, at], first_peer[p])
                following[p].start()
        return following

    def low_second(p, copy):
        copy.wait()
        low1[p] = low0[p] + lg1[p]
        following = send(p, 7, low1.at[p], lg2.at[p], first_peer[p])
        following.start()
        return following

    def low_third(p, copy):
        copy.wait()
        low2[p] = low1[p] + lg2[p]
        following = send(p, 8, low2.at[p], lg3.at[p], second_peer[p])
        following.start()
        return following

    def low_last(p, copy):
        copy.wait()
        low3[p] = low2[p] + lg3[p]
        copies = []
        for k in range(3):
            copies.append(send(p, 9 + k, low3.at[p], lg4.at[p, k], z_peers[k]))
            copies[-1].start()
        return copies

    def along_second(p, copy):
        copy.wait()
        following = []
        for part in range(2):
            for slot in (2 * part, 2 * part + 1):
                sent3[p, slot] = (kept1[p, 4 + slot] + got2[p, 4 + slot].astype(F32)).astype(BF16)
            at = pl.ds(2 * part, 2)
            following.append(
                send(p, 2 + 14 * part, sent3.at[p, at], got3.at[p, at], second_peer[p])
            )
            following[-1].start()
        return following

    def keep_second(p, copy):
        copy.wait()
        for slot in range(4):
            kept2[p, slot] = kept1[p, slot] + got2[p, slot].astype(F32)

    def along_z(p, part, copy):
        copy.wait()
        copies = []
        for slot in (0, 1) if part == 0 else (2,):
            sent4[p, slot] = (kept2[p, slot] + got3[p, slot].astype(F32)).astype(BF16)
            copies.append(
                send(p, 3 + slot, sent4.at[p, slot], got4.at[p, slot], z_slot_peers[slot])
            )
            copies[-1].start()
        return copies

    def finish(p, low_copies):
        for copy in low_copies:
            copy.wait()
        low = unfold(low3[p] + lg4[p, 0] + (lg4[p, 1] + lg4[p, 2]))
        low = low.astype(BF16).astype(F32)
        pick = picks[p * half : (p + 1) * half, :rank]
        total = kept2[p, 3] + got3[p, 3].astype(F32)
        for a in range(count):
            chosen = jnp.where(pick == a, low, 0.0).astype(BF16)
            total = total + jnp.dot(chosen, up[a], preferred_element_type=F32)
        return total

    pieces = range(PIECES)
    lax.fori_loop(0, chunks, attend, 0)
    pl.semaphore_wait(barrier, len(peers))
    w_load.wait()
    crossing = {}
    crossing[1, 1] = far(1, 1)
    down_load.wait()
    low = [low_part(p) for p in pieces]
    for key in ((1, 0), (0, 1), (0, 0)):
        crossing[key] = far(*key)
    early = near(1, 1, crossing[1, 1])
    low = [low_second(p, low[p]) for p in pieces]
    late = [None] * PIECES
    late[0] = near(1, 0, crossing[1, 0])[0]
    late[1] = near(0, 1, crossing[0, 1])[1]
    low = [low_third(p, low[p]) for p in pieces]
    near(0, 0, crossing[0, 0])
    turned = [along_second(p, early[p]) for p in pieces]
    low = [low_last(p, low[p]) for p in pieces]
    for p in pieces:
        keep_second(p, late[p])
    last = [along_z(p, 0, turned[p][0]) for p in pieces]
    for p in pieces:
        last[p] = last[p] + along_z(p, 1, turned[p][1])
    up_load.wait()
    totals = [finish(p, low[p]) for p in pieces]
    for p in pieces:
        for copy in last[p]:
            copy.wait()
        for slot in range(3):
            totals[p] = totals[p] + got4[p, slot].astype(F32)
    out_ref[...] = jnp.transpose(jnp.concatenate(totals, axis=0)).astype(BF16)


def body(
    queries,
    cache,
    lengths,
    request_adapter_index,
    output_projection_weight,
    adapter_down_weight,
    adapter_up_weight,
):
    downs, ups = (
        lax.all_gather(adapter_down_weight, "dp", axis=0, tiled=True),
        lax.all_gather(adapter_up_weight, "dp", axis=0, tiled=True),
    )
    rows = queries.shape[0]
    half = rows // PIECES
    chunks = rows // CHUNK
    slots = cache.shape[2]
    width = ups.shape[2]
    downs = jnp.transpose(downs, (0, 2, 1))
    rank = downs.shape[1]
    low = (PIECES, half // 2, 2 * rank)

    def blocks(n, kind=BF16):
        return pltpu.VMEM((PIECES, n, half, width), kind)

    vmem = pl.BlockSpec(memory_space=pltpu.VMEM)
    hbm = pl.BlockSpec(memory_space=pltpu.HBM)
    return pl.pallas_call(
        kernel,
        out_shape=jax.ShapeDtypeStruct((width, rows), BF16),
        in_specs=[hbm] * 7,
        out_specs=vmem,
        scratch_shapes=[
            pltpu.VMEM(queries.shape, BF16),
            pltpu.VMEM((1, rows), jnp.int32),
            pltpu.VMEM((1, rows), jnp.int32),
            pltpu.VMEM(cache.shape[1:], BF16),
            pltpu.VMEM(output_projection_weight.shape, BF16),
            pltpu.VMEM(downs.shape, BF16),
            pltpu.VMEM(ups.shape, BF16),
            pltpu.VMEM((rows, slots), F32),
            pltpu.VMEM((rows, width), F32),
            pltpu.VMEM((rows, queries.shape[1]), BF16),
            blocks(16), blocks(16, F32), blocks(16),
            blocks(8), blocks(8, F32), blocks(8),
            blocks(4), blocks(4, F32), blocks(4),
            blocks(3), blocks(3),
            pltpu.VMEM(low, F32), pltpu.VMEM(low, F32), pltpu.VMEM(low, F32), pltpu.VMEM(low, F32),
            pltpu.VMEM(low, F32), pltpu.VMEM(low, F32), pltpu.VMEM(low, F32),
            pltpu.VMEM((PIECES, 3) + low[1:], F32),
            pltpu.SemaphoreType.DMA((chunks + 6,)),
            pltpu.SemaphoreType.DMA((PIECES, 17)),
            pltpu.SemaphoreType.DMA((PIECES, 17)),
        ],
        compiler_params=pltpu.CompilerParams(
            collective_id=0, has_side_effects=True, vmem_limit_bytes=56 * 1024 * 1024
        ),
    )(
        queries,
        lengths.reshape(1, rows),
        request_adapter_index.reshape(1, rows),
        cache,
        output_projection_weight,
        downs,
        ups,
    )


def solution(mesh):
    return jax.shard_map(
        body,
        mesh=mesh,
        in_specs=(
            P(("groups", "dp"), "tensor"),
            P("tensor", ("groups", "dp"), None, None),
            P(("groups", "dp")),
            P(("groups", "dp")),
            P("tensor", None),
            P(("groups", "dp"), "tensor", None),
            P(("groups", "dp"), None, "tensor"),
        ),
        out_specs=P("tensor", ("groups", "dp")),
        check_vma=False,
    )
```

```python
import math

import jax
import jax.numpy as jnp
from jax import lax
from jax.experimental import pallas as pl
from jax.experimental.pallas import tpu as pltpu
from jax.sharding import PartitionSpec as P

HEAD = 128
PIECES = 2
CHUNK = 16
MESH = pl.DeviceIdType.MESH
F32 = jnp.float32
BF16 = jnp.bfloat16
NEG = -1e30


def kernel(
    q_hbm, len_hbm, idx_hbm, cache_hbm, w_hbm, down_hbm, up_hbm, out_ref,
    q_ref, len_ref, idx_ref, cache, w, down, up, lens, picks, att,
    sent1, own, got1, sent2, kept1, got2, sent3, kept2, got3, sent4, got4,
    low0, low1, low2, low3, lg1, lg2, lg3, lg4,
    load_sem, send_sem, recv_sem,
):
    rows = q_hbm.shape[0]
    half = rows // PIECES
    chunks = rows // CHUNK
    slots = cache.shape[1]
    count = down.shape[0]
    rank = down.shape[1]
    out_width = up.shape[2]

    me = lax.axis_index("tensor")
    core = me % 2
    xx = (me // 2) % 2
    yy = (me // 4) % 2
    zz = me // 8
    core_peer = me + 1 - 2 * core
    x_peer = me + 2 - 4 * xx
    y_peer = me + 4 - 8 * yy
    z_others = (zz + 1 - 2 * (zz % 2), (zz + 2) % 4, 3 - zz)
    z_peers = tuple(me + 8 * (other - zz) for other in z_others)
    peers = (core_peer, x_peer, y_peer) + z_peers

    cache_loads = [
        pltpu.make_async_copy(
            cache_hbm.at[0, pl.ds(c * CHUNK, CHUNK)],
            cache.at[pl.ds(c * CHUNK, CHUNK)],
            load_sem.at[c],
        )
        for c in range(chunks)
    ]
    down_load = pltpu.make_async_copy(down_hbm, down, load_sem.at[chunks])
    up_load = pltpu.make_async_copy(up_hbm, up, load_sem.at[chunks + 1])
    w_load = pltpu.make_async_copy(w_hbm, w, load_sem.at[chunks + 2])
    small_loads = [
        pltpu.make_async_copy(src, dst, load_sem.at[chunks + 3 + i])
        for i, (src, dst) in enumerate(((q_hbm, q_ref), (len_hbm, len_ref), (idx_hbm, idx_ref)))
    ]
    for load in small_loads:
        load.start()
    for c in range(chunks // 2):
        cache_loads[c].start()
    down_load.start()
    w_load.start()
    for c in range(chunks // 2, chunks):
        cache_loads[c].start()
    up_load.start()

    barrier = pltpu.get_barrier_semaphore()
    for peer in peers:
        pl.semaphore_signal(barrier, inc=1, device_id={"tensor": peer}, device_id_type=MESH)

    def send(p, step, src, dst, peer):
        return pltpu.make_async_remote_copy(
            src_ref=src,
            dst_ref=dst,
            send_sem=send_sem.at[p, step],
            recv_sem=recv_sem.at[p, step],
            device_id={"tensor": peer},
            device_id_type=MESH,
        )

    for load in small_loads:
        load.wait()
    lens[...] = jnp.transpose(jnp.broadcast_to(len_ref[...].astype(F32), (slots, rows)))
    picks[...] = jnp.transpose(jnp.broadcast_to(idx_ref[...].astype(F32), (out_width, rows)))

    row_of = lax.broadcasted_iota(jnp.int32, (2 * CHUNK, slots), 0) % CHUNK
    slot_of = lax.broadcasted_iota(jnp.int32, (2 * CHUNK, slots), 1).astype(F32)
    scale = 1.0 / math.sqrt(HEAD)

    def attend(c, carry):
        at = pl.multiple_of(c * CHUNK, CHUNK)
        pltpu.make_async_copy(
            cache_hbm.at[0, pl.ds(at, CHUNK)], cache.at[pl.ds(at, CHUNK)], load_sem.at[c]
        ).wait()
        block = cache[pl.ds(at, CHUNK)].reshape(CHUNK * slots, 2 * HEAD)
        q = q_ref[pl.ds(at, CHUNK), :]
        q = jnp.concatenate([q[:, :HEAD], q[:, HEAD:]], axis=0)
        raw = lax.dot_general(
            q, block[:, :HEAD], (((1,), (1,)), ((), ())), preferred_element_type=F32
        )
        scores = raw[:, :slots]
        for r in range(1, CHUNK):
            scores = jnp.where(row_of == r, raw[:, r * slots : (r + 1) * slots], scores)
        live = lens[pl.ds(at, CHUNK), :]
        live = jnp.concatenate([live, live], axis=0)
        scores = jnp.where(slot_of < live, scores * scale, NEG)
        top = jnp.max(scores, axis=-1, keepdims=True)
        expd = jnp.exp(scores - top)
        weights = expd / jnp.sum(expd, axis=-1, keepdims=True)
        spread = jnp.concatenate(
            [jnp.where(row_of == r, weights, 0.0).astype(BF16) for r in range(CHUNK)], axis=1
        )
        mixed = jnp.dot(spread, block[:, HEAD:], preferred_element_type=F32).astype(BF16)
        att[pl.ds(at, CHUNK), :HEAD] = mixed[:CHUNK]
        att[pl.ds(at, CHUNK), HEAD:] = mixed[CHUNK:]
        return carry

    def fold(low):
        return jnp.concatenate([low[: half // 2], low[half // 2 :]], axis=1)

    def unfold(low):
        return jnp.concatenate([low[:, :rank], low[:, rank:]], axis=0)

    first_peer = (x_peer, y_peer)
    second_peer = (y_peer, x_peer)
    z_order = (z_others[1], z_others[2], z_others[0], zz)
    z_slot_peers = (z_peers[1], z_peers[2], z_peers[0])

    def group_of(p, dx, dy):
        return dx * 2 + dy if p == 0 else dy * 2 + dx

    def low_part(p):
        piece = att[p * half : (p + 1) * half, :].astype(F32)
        pick = picks[p * half : (p + 1) * half, :]
        total = jnp.zeros((half, rank), F32)
        for a in range(count):
            chosen = jnp.where(pick == a, piece, 0.0).astype(BF16)
            total = total + lax.dot_general(
                chosen, down[a], (((1,), (1,)), ((), ())), preferred_element_type=F32
            )
        low0[p] = fold(total)
        copy = send(p, 6, low0.at[p], lg1.at[p], core_peer)
        copy.start()
        return copy

    def product(dx, dy, side, slot):
        x_at = xx + dx * (1 - 2 * xx)
        y_at = yy + dy * (1 - 2 * yy)
        index = z_order[slot] * 8 + y_at * 4 + x_at * 2 + side
        columns = pl.ds(pl.multiple_of(index * out_width, out_width), out_width)
        return jnp.dot(att[...], w[:, columns], preferred_element_type=F32)

    def far(dx, dy):
        places = (group_of(0, dx, dy), group_of(1, dx, dy))
        for slot in range(4):
            block = product(dx, dy, 1 - core, slot).astype(BF16)
            for p in range(PIECES):
                sent1[p, places[p] * 4 + slot] = block[p * half : (p + 1) * half]
        copies = []
        for p in range(PIECES):
            at = pl.ds(places[p] * 4, 4)
            copies.append(send(p, 12 + places[p], sent1.at[p, at], got1.at[p, at], core_peer))
            copies[-1].start()
        return copies

    def near(dx, dy, copies):
        places = (group_of(0, dx, dy), group_of(1, dx, dy))
        for slot in range(4):
            block = product(dx, dy, core, slot)
            for p in range(PIECES):
                own[p, places[p] * 4 + slot] = block[p * half : (p + 1) * half]
        following = [None] * PIECES
        for p in range(PIECES):
            place = places[p]
            copies[p].wait()
            to = (place % 2) * 4
            for slot in range(4):
                total = own[p, place * 4 + slot] + got1[p, place * 4 + slot].astype(F32)
                if place >= 2:
                    sent2[p, to + slot] = total.astype(BF16)
                else:
                    kept1[p, to + slot] = total
            if place >= 2:
                at = pl.ds(to, 4)
                following[p] = send(p, place % 2, sent2.at[p, at], got2.at[p, at], first_peer[p])
                following[p].start()
        return following

    def low_second(p, copy):
        copy.wait()
        low1[p] = low0[p] + lg1[p]
        following = send(p, 7, low1.at[p], lg2.at[p], first_peer[p])
        following.start()
        return following

    def low_third(p, copy):
        copy.wait()
        low2[p] = low1[p] + lg2[p]
        following = send(p, 8, low2.at[p], lg3.at[p], second_peer[p])
        following.start()
        return following

    def low_last(p, copy):
        copy.wait()
        low3[p] = low2[p] + lg3[p]
        copies = []
        for k in range(3):
            copies.append(send(p, 9 + k, low3.at[p], lg4.at[p, k], z_peers[k]))
            copies[-1].start()
        return copies

    def along_second(p, copy):
        copy.wait()
        following = []
        for part in range(2):
            for slot in (2 * part, 2 * part + 1):
                sent3[p, slot] = (kept1[p, 4 + slot] + got2[p, 4 + slot].astype(F32)).astype(BF16)
            at = pl.ds(2 * part, 2)
            following.append(
                send(p, 2 + 14 * part, sent3.at[p, at], got3.at[p, at], second_peer[p])
            )
            following[-1].start()
        return following

    def keep_second(p, copy):
        copy.wait()
        for slot in range(4):
            kept2[p, slot] = kept1[p, slot] + got2[p, slot].astype(F32)

    def along_z(p, part, copy):
        copy.wait()
        copies = []
        for slot in (0, 1) if part == 0 else (2,):
            sent4[p, slot] = (kept2[p, slot] + got3[p, slot].astype(F32)).astype(BF16)
            copies.append(
                send(p, 3 + slot, sent4.at[p, slot], got4.at[p, slot], z_slot_peers[slot])
            )
            copies[-1].start()
        return copies

    def finish(p, low_copies):
        for copy in low_copies:
            copy.wait()
        low = unfold(low3[p] + lg4[p, 0] + (lg4[p, 1] + lg4[p, 2]))
        low = low.astype(BF16).astype(F32)
        pick = picks[p * half : (p + 1) * half, :rank]
        total = kept2[p, 3] + got3[p, 3].astype(F32)
        for a in range(count):
            chosen = jnp.where(pick == a, low, 0.0).astype(BF16)
            total = total + jnp.dot(chosen, up[a], preferred_element_type=F32)
        return total

    pieces = range(PIECES)
    lax.fori_loop(0, chunks, attend, 0)
    pl.semaphore_wait(barrier, len(peers))
    down_load.wait()
    low = [low_part(p) for p in pieces]
    w_load.wait()
    crossing = {}
    late = [None] * PIECES
    crossing[1, 1] = far(1, 1)
    crossing[1, 0] = far(1, 0)
    low = [low_second(p, low[p]) for p in pieces]
    early = near(1, 1, crossing[1, 1])
    crossing[0, 1] = far(0, 1)
    crossing[0, 0] = far(0, 0)
    low = [low_third(p, low[p]) for p in pieces]
    late[0] = near(1, 0, crossing[1, 0])[0]
    late[1] = near(0, 1, crossing[0, 1])[1]
    near(0, 0, crossing[0, 0])
    low = [low_last(p, low[p]) for p in pieces]
    turned = [along_second(p, early[p]) for p in pieces]
    for p in pieces:
        keep_second(p, late[p])
    last = [along_z(p, 0, turned[p][0]) for p in pieces]
    for p in pieces:
        last[p] = last[p] + along_z(p, 1, turned[p][1])
    up_load.wait()
    totals = [finish(p, low[p]) for p in pieces]
    for p in pieces:
        for copy in last[p]:
            copy.wait()
        for slot in range(3):
            totals[p] = totals[p] + got4[p, slot].astype(F32)
    out_ref[...] = jnp.transpose(jnp.concatenate(totals, axis=0)).astype(BF16)


def body(
    queries,
    cache,
    lengths,
    request_adapter_index,
    output_projection_weight,
    adapter_down_weight,
    adapter_up_weight,
):
    downs, ups = (
        lax.all_gather(adapter_down_weight, "dp", axis=0, tiled=True),
        lax.all_gather(adapter_up_weight, "dp", axis=0, tiled=True),
    )
    rows = queries.shape[0]
    half = rows // PIECES
    chunks = rows // CHUNK
    slots = cache.shape[2]
    width = ups.shape[2]
    downs = jnp.transpose(downs, (0, 2, 1))
    rank = downs.shape[1]
    low = (PIECES, half // 2, 2 * rank)

    def blocks(n, kind=BF16):
        return pltpu.VMEM((PIECES, n, half, width), kind)

    vmem = pl.BlockSpec(memory_space=pltpu.VMEM)
    hbm = pl.BlockSpec(memory_space=pltpu.HBM)
    return pl.pallas_call(
        kernel,
        out_shape=jax.ShapeDtypeStruct((width, rows), BF16),
        in_specs=[hbm] * 7,
        out_specs=vmem,
        scratch_shapes=[
            pltpu.VMEM(queries.shape, BF16),
            pltpu.VMEM((1, rows), jnp.int32),
            pltpu.VMEM((1, rows), jnp.int32),
            pltpu.VMEM(cache.shape[1:], BF16),
            pltpu.VMEM(output_projection_weight.shape, BF16),
            pltpu.VMEM(downs.shape, BF16),
            pltpu.VMEM(ups.shape, BF16),
            pltpu.VMEM((rows, slots), F32),
            pltpu.VMEM((rows, width), F32),
            pltpu.VMEM((rows, queries.shape[1]), BF16),
            blocks(16), blocks(16, F32), blocks(16),
            blocks(8), blocks(8, F32), blocks(8),
            blocks(4), blocks(4, F32), blocks(4),
            blocks(3), blocks(3),
            pltpu.VMEM(low, F32), pltpu.VMEM(low, F32), pltpu.VMEM(low, F32), pltpu.VMEM(low, F32),
            pltpu.VMEM(low, F32), pltpu.VMEM(low, F32), pltpu.VMEM(low, F32),
            pltpu.VMEM((PIECES, 3) + low[1:], F32),
            pltpu.SemaphoreType.DMA((chunks + 6,)),
            pltpu.SemaphoreType.DMA((PIECES, 17)),
            pltpu.SemaphoreType.DMA((PIECES, 17)),
        ],
        compiler_params=pltpu.CompilerParams(
            collective_id=0, has_side_effects=True, vmem_limit_bytes=56 * 1024 * 1024
        ),
    )(
        queries,
        lengths.reshape(1, rows),
        request_adapter_index.reshape(1, rows),
        cache,
        output_projection_weight,
        downs,
        ups,
    )


def solution(mesh):
    return jax.shard_map(
        body,
        mesh=mesh,
        in_specs=(
            P(("groups", "dp"), "tensor"),
            P("tensor", ("groups", "dp"), None, None),
            P(("groups", "dp")),
            P(("groups", "dp")),
            P("tensor", None),
            P(("groups", "dp"), "tensor", None),
            P(("groups", "dp"), None, "tensor"),
        ),
        out_specs=P("tensor", ("groups", "dp")),
        check_vma=False,
    )
```

```python
import math

import jax
import jax.numpy as jnp
from jax import lax
from jax.experimental import pallas as pl
from jax.experimental.pallas import tpu as pltpu
from jax.sharding import PartitionSpec as P

HEAD = 128
PIECES = 2
CHUNK = 16
MESH = pl.DeviceIdType.MESH
F32 = jnp.float32
BF16 = jnp.bfloat16
NEG = -1e30


def kernel(
    q_hbm, len_hbm, idx_hbm, cache_hbm, w_hbm, down_hbm, up_hbm, out_ref,
    q_ref, len_ref, idx_ref, cache, w, down, up, lens, picks, att,
    sent1, own, got1, sent2, kept1, got2, sent3, kept2, got3, sent4, got4,
    low0, low1, low2, low3, lg1, lg2, lg3, lg4,
    load_sem, send_sem, recv_sem,
):
    rows = q_hbm.shape[0]
    half = rows // PIECES
    chunks = rows // CHUNK
    slots = cache.shape[1]
    count = down.shape[0]
    rank = down.shape[1]
    out_width = up.shape[2]

    me = lax.axis_index("tensor")
    core = me % 2
    xx = (me // 2) % 2
    yy = (me // 4) % 2
    zz = me // 8
    core_peer = me + 1 - 2 * core
    x_peer = me + 2 - 4 * xx
    y_peer = me + 4 - 8 * yy
    z_others = (zz + 1 - 2 * (zz % 2), (zz + 2) % 4, 3 - zz)
    z_peers = tuple(me + 8 * (other - zz) for other in z_others)
    peers = (core_peer, x_peer, y_peer) + z_peers

    cache_loads = [
        pltpu.make_async_copy(
            cache_hbm.at[0, pl.ds(c * CHUNK, CHUNK)],
            cache.at[pl.ds(c * CHUNK, CHUNK)],
            load_sem.at[c],
        )
        for c in range(chunks)
    ]
    down_load = pltpu.make_async_copy(down_hbm, down, load_sem.at[chunks])
    up_load = pltpu.make_async_copy(up_hbm, up, load_sem.at[chunks + 1])
    quarter = w.shape[0] // 4
    w_loads = [
        pltpu.make_async_copy(
            w_hbm.at[pl.ds(i * quarter, quarter)],
            w.at[pl.ds(i * quarter, quarter)],
            load_sem.at[chunks + (2, 6, 7, 8)[i]],
        )
        for i in range(4)
    ]
    small_loads = [
        pltpu.make_async_copy(src, dst, load_sem.at[chunks + 3 + i])
        for i, (src, dst) in enumerate(((q_hbm, q_ref), (len_hbm, len_ref), (idx_hbm, idx_ref)))
    ]
    for load in small_loads:
        load.start()
    for c in range(chunks // 2):
        cache_loads[c].start()
    for c in range(chunks // 2, chunks):
        cache_loads[c].start()
    down_load.start()
    for load in w_loads:
        load.start()
    up_load.start()

    barrier = pltpu.get_barrier_semaphore()
    for peer in peers:
        pl.semaphore_signal(barrier, inc=1, device_id={"tensor": peer}, device_id_type=MESH)

    def send(p, step, src, dst, peer):
        return pltpu.make_async_remote_copy(
            src_ref=src,
            dst_ref=dst,
            send_sem=send_sem.at[p, step],
            recv_sem=recv_sem.at[p, step],
            device_id={"tensor": peer},
            device_id_type=MESH,
        )

    for load in small_loads:
        load.wait()
    lens[...] = jnp.transpose(jnp.broadcast_to(len_ref[...].astype(F32), (slots, rows)))
    picks[...] = jnp.transpose(jnp.broadcast_to(idx_ref[...].astype(F32), (out_width, rows)))

    row_of = lax.broadcasted_iota(jnp.int32, (2 * CHUNK, slots), 0) % CHUNK
    slot_of = lax.broadcasted_iota(jnp.int32, (2 * CHUNK, slots), 1).astype(F32)
    scale = 1.0 / math.sqrt(HEAD)

    def attend(c, carry):
        at = pl.multiple_of(c * CHUNK, CHUNK)
        pltpu.make_async_copy(
            cache_hbm.at[0, pl.ds(at, CHUNK)], cache.at[pl.ds(at, CHUNK)], load_sem.at[c]
        ).wait()
        block = cache[pl.ds(at, CHUNK)].reshape(CHUNK * slots, 2 * HEAD)
        q = q_ref[pl.ds(at, CHUNK), :]
        q = jnp.concatenate([q[:, :HEAD], q[:, HEAD:]], axis=0)
        raw = lax.dot_general(
            q, block[:, :HEAD], (((1,), (1,)), ((), ())), preferred_element_type=F32
        )
        scores = raw[:, :slots]
        for r in range(1, CHUNK):
            scores = jnp.where(row_of == r, raw[:, r * slots : (r + 1) * slots], scores)
        live = lens[pl.ds(at, CHUNK), :]
        live = jnp.concatenate([live, live], axis=0)
        scores = jnp.where(slot_of < live, scores * scale, NEG)
        top = jnp.max(scores, axis=-1, keepdims=True)
        expd = jnp.exp(scores - top)
        weights = expd / jnp.sum(expd, axis=-1, keepdims=True)
        spread = jnp.concatenate(
            [jnp.where(row_of == r, weights, 0.0).astype(BF16) for r in range(CHUNK)], axis=1
        )
        mixed = jnp.dot(spread, block[:, HEAD:], preferred_element_type=F32).astype(BF16)
        att[pl.ds(at, CHUNK), :HEAD] = mixed[:CHUNK]
        att[pl.ds(at, CHUNK), HEAD:] = mixed[CHUNK:]
        return carry

    def fold(low):
        return jnp.concatenate([low[: half // 2], low[half // 2 :]], axis=1)

    def unfold(low):
        return jnp.concatenate([low[:, :rank], low[:, rank:]], axis=0)

    first_peer = (x_peer, y_peer)
    second_peer = (y_peer, x_peer)
    z_order = (z_others[1], z_others[2], z_others[0], zz)
    z_slot_peers = (z_peers[1], z_peers[2], z_peers[0])

    def group_of(p, dx, dy):
        return dx * 2 + dy if p == 0 else dy * 2 + dx

    def low_part(p):
        piece = att[p * half : (p + 1) * half, :].astype(F32)
        pick = picks[p * half : (p + 1) * half, :]
        total = jnp.zeros((half, rank), F32)
        for a in range(count):
            chosen = jnp.where(pick == a, piece, 0.0).astype(BF16)
            total = total + lax.dot_general(
                chosen, down[a], (((1,), (1,)), ((), ())), preferred_element_type=F32
            )
        low0[p] = fold(total)
        copy = send(p, 6, low0.at[p], lg1.at[p], core_peer)
        copy.start()
        return copy

    def product(dx, dy, side, slot):
        x_at = xx + dx * (1 - 2 * xx)
        y_at = yy + dy * (1 - 2 * yy)
        index = z_order[slot] * 8 + y_at * 4 + x_at * 2 + side
        columns = pl.ds(pl.multiple_of(index * out_width, out_width), out_width)
        return jnp.dot(att[...], w[:, columns], preferred_element_type=F32)

    def far(dx, dy):
        places = (group_of(0, dx, dy), group_of(1, dx, dy))
        for slot in range(4):
            block = product(dx, dy, 1 - core, slot).astype(BF16)
            for p in range(PIECES):
                sent1[p, places[p] * 4 + slot] = block[p * half : (p + 1) * half]
        copies = []
        for p in range(PIECES):
            at = pl.ds(places[p] * 4, 4)
            copies.append(send(p, 12 + places[p], sent1.at[p, at], got1.at[p, at], core_peer))
            copies[-1].start()
        return copies

    def near(dx, dy, copies):
        places = (group_of(0, dx, dy), group_of(1, dx, dy))
        for slot in range(4):
            block = product(dx, dy, core, slot)
            for p in range(PIECES):
                own[p, places[p] * 4 + slot] = block[p * half : (p + 1) * half]
        following = [None] * PIECES
        for p in range(PIECES):
            place = places[p]
            copies[p].wait()
            to = (place % 2) * 4
            for slot in range(4):
                total = own[p, place * 4 + slot] + got1[p, place * 4 + slot].astype(F32)
                if place >= 2:
                    sent2[p, to + slot] = total.astype(BF16)
                else:
                    kept1[p, to + slot] = total
            if place >= 2:
                at = pl.ds(to, 4)
                following[p] = send(p, place % 2, sent2.at[p, at], got2.at[p, at], first_peer[p])
                following[p].start()
        return following

    def low_second(p, copy):
        copy.wait()
        low1[p] = low0[p] + lg1[p]
        following = send(p, 7, low1.at[p], lg2.at[p], first_peer[p])
        following.start()
        return following

    def low_third(p, copy):
        copy.wait()
        low2[p] = low1[p] + lg2[p]
        following = send(p, 8, low2.at[p], lg3.at[p], second_peer[p])
        following.start()
        return following

    def low_last(p, copy):
        copy.wait()
        low3[p] = low2[p] + lg3[p]
        copies = []
        for k in range(3):
            copies.append(send(p, 9 + k, low3.at[p], lg4.at[p, k], z_peers[k]))
            copies[-1].start()
        return copies

    def along_second(p, copy):
        copy.wait()
        following = []
        for part in range(2):
            for slot in (2 * part, 2 * part + 1):
                sent3[p, slot] = (kept1[p, 4 + slot] + got2[p, 4 + slot].astype(F32)).astype(BF16)
            at = pl.ds(2 * part, 2)
            following.append(
                send(p, 2 + 14 * part, sent3.at[p, at], got3.at[p, at], second_peer[p])
            )
            following[-1].start()
        return following

    def keep_second(p, copy):
        copy.wait()
        for slot in range(4):
            kept2[p, slot] = kept1[p, slot] + got2[p, slot].astype(F32)

    def along_z(p, part, copy):
        copy.wait()
        copies = []
        for slot in (0, 1) if part == 0 else (2,):
            sent4[p, slot] = (kept2[p, slot] + got3[p, slot].astype(F32)).astype(BF16)
            copies.append(
                send(p, 3 + slot, sent4.at[p, slot], got4.at[p, slot], z_slot_peers[slot])
            )
            copies[-1].start()
        return copies

    def finish(p, low_copies):
        for copy in low_copies:
            copy.wait()
        low = unfold(low3[p] + lg4[p, 0] + (lg4[p, 1] + lg4[p, 2]))
        low = low.astype(BF16).astype(F32)
        pick = picks[p * half : (p + 1) * half, :rank]
        total = kept2[p, 3] + got3[p, 3].astype(F32)
        for a in range(count):
            chosen = jnp.where(pick == a, low, 0.0).astype(BF16)
            total = total + jnp.dot(chosen, up[a], preferred_element_type=F32)
        return total

    pieces = range(PIECES)
    lax.fori_loop(0, chunks, attend, 0, unroll=2)
    pl.semaphore_wait(barrier, len(peers))
    down_load.wait()
    low = [low_part(p) for p in pieces]
    for load in w_loads:
        load.wait()
    crossing = {}
    late = [None] * PIECES
    crossing[1, 1] = far(1, 1)
    crossing[1, 0] = far(1, 0)
    low = [low_second(p, low[p]) for p in pieces]
    early = near(1, 1, crossing[1, 1])
    crossing[0, 1] = far(0, 1)
    crossing[0, 0] = far(0, 0)
    low = [low_third(p, low[p]) for p in pieces]
    late[0] = near(1, 0, crossing[1, 0])[0]
    late[1] = near(0, 1, crossing[0, 1])[1]
    near(0, 0, crossing[0, 0])
    low = [low_last(p, low[p]) for p in pieces]
    turned = [along_second(p, early[p]) for p in pieces]
    for p in pieces:
        keep_second(p, late[p])
    last = [along_z(p, 0, turned[p][0]) for p in pieces]
    for p in pieces:
        last[p] = last[p] + along_z(p, 1, turned[p][1])
    up_load.wait()
    totals = [finish(p, low[p]) for p in pieces]
    for p in pieces:
        for copy in last[p]:
            copy.wait()
        for slot in range(3):
            totals[p] = totals[p] + got4[p, slot].astype(F32)
    out_ref[...] = jnp.transpose(jnp.concatenate(totals, axis=0)).astype(BF16)


def body(
    queries,
    cache,
    lengths,
    request_adapter_index,
    output_projection_weight,
    adapter_down_weight,
    adapter_up_weight,
):
    downs, ups = (
        lax.all_gather(adapter_down_weight, "dp", axis=0, tiled=True),
        lax.all_gather(adapter_up_weight, "dp", axis=0, tiled=True),
    )
    rows = queries.shape[0]
    half = rows // PIECES
    chunks = rows // CHUNK
    slots = cache.shape[2]
    width = ups.shape[2]
    downs = jnp.transpose(downs, (0, 2, 1))
    rank = downs.shape[1]
    low = (PIECES, half // 2, 2 * rank)

    def blocks(n, kind=BF16):
        return pltpu.VMEM((PIECES, n, half, width), kind)

    vmem = pl.BlockSpec(memory_space=pltpu.VMEM)
    hbm = pl.BlockSpec(memory_space=pltpu.HBM)
    return pl.pallas_call(
        kernel,
        out_shape=jax.ShapeDtypeStruct((width, rows), BF16),
        in_specs=[hbm] * 7,
        out_specs=vmem,
        scratch_shapes=[
            pltpu.VMEM(queries.shape, BF16),
            pltpu.VMEM((1, rows), jnp.int32),
            pltpu.VMEM((1, rows), jnp.int32),
            pltpu.VMEM(cache.shape[1:], BF16),
            pltpu.VMEM(output_projection_weight.shape, BF16),
            pltpu.VMEM(downs.shape, BF16),
            pltpu.VMEM(ups.shape, BF16),
            pltpu.VMEM((rows, slots), F32),
            pltpu.VMEM((rows, width), F32),
            pltpu.VMEM((rows, queries.shape[1]), BF16),
            blocks(16), blocks(16, F32), blocks(16),
            blocks(8), blocks(8, F32), blocks(8),
            blocks(4), blocks(4, F32), blocks(4),
            blocks(3), blocks(3),
            pltpu.VMEM(low, F32), pltpu.VMEM(low, F32), pltpu.VMEM(low, F32), pltpu.VMEM(low, F32),
            pltpu.VMEM(low, F32), pltpu.VMEM(low, F32), pltpu.VMEM(low, F32),
            pltpu.VMEM((PIECES, 3) + low[1:], F32),
            pltpu.SemaphoreType.DMA((chunks + 9,)),
            pltpu.SemaphoreType.DMA((PIECES, 17)),
            pltpu.SemaphoreType.DMA((PIECES, 17)),
        ],
        compiler_params=pltpu.CompilerParams(
            collective_id=0, has_side_effects=True, vmem_limit_bytes=56 * 1024 * 1024
        ),
    )(
        queries,
        lengths.reshape(1, rows),
        request_adapter_index.reshape(1, rows),
        cache,
        output_projection_weight,
        downs,
        ups,
    )


def solution(mesh):
    return jax.shard_map(
        body,
        mesh=mesh,
        in_specs=(
            P(("groups", "dp"), "tensor"),
            P("tensor", ("groups", "dp"), None, None),
            P(("groups", "dp")),
            P(("groups", "dp")),
            P("tensor", None),
            P(("groups", "dp"), "tensor", None),
            P(("groups", "dp"), None, "tensor"),
        ),
        out_specs=P("tensor", ("groups", "dp")),
        check_vma=False,
    )
```
